256 devices in a mesh: rcv: 64 (over x_lo, y, z), seg: 4 (over x_hi, core).
Axes of the slice: x: 4 (x_hi: 2, x_lo: 2; x = x_hi * 2 + x_lo), y: 4, z: 8, core: 2. Of those that a mesh axis runs over, the one named last changes fastest.
Arguments:
- traces: bfloat16 [8, 8, 1024, 2048], P('seg', None, 'rcv'), may hold values from -6 to 6
- valid_flags: int32 [8], replicated, may hold values from 0 to 1, as said below
- source_block: int32 [4], replicated, may hold values from 0 to 63
Outputs:
- correlations: float32 [4, 16, 1024, 512], P(None, 'seg', 'rcv')
The draws below stay inside these ranges and needn't reach their ends.
Inputs may be any that keep to these rules, and one draw needn't show every extreme that they name: `valid_flags`: at least one segment is valid and at least one is not.
All inputs are finite; a program needn't handle non-finite values.
Results may differ from the reference program's by a relative error of at most 0.0055.
Values may be sent and summed in bfloat16 or wider, within the bound.
A program may use at most 64 MiB of HBM per device.

```python
import math
import jax
import jax.numpy as jnp
from jax import lax

NFFT = 2048
LAGS = 512
FR = 8
SB = 16
STEPS = 4
S_DEV = 2
SEGMENTS = 8
CHANNELS = 1024
N_SEG = 4


def draw_valid_flags(key, part):
    key = jax.random.fold_in(key, 7)
    key_bits, key_anchor, key_gap = jax.random.split(key, 3)
    levels = jax.random.randint(key_bits, (SEGMENTS,), 0, 2)
    anchor = jax.random.randint(key_anchor, (), 0, SEGMENTS)
    gap = jax.random.randint(key_gap, (), 1, SEGMENTS)
    dropped = (anchor + gap) % SEGMENTS
    positions = jnp.arange(SEGMENTS, dtype=jnp.int32)
    planted = (positions == anchor).astype(jnp.int32)
    removed = (positions == dropped).astype(jnp.int32)
    return jnp.maximum(levels, planted) * (1 - removed)


def touch_ends(values, key, low, high):
    longest = values.shape.index(max(values.shape))
    spots = []
    for shift in (0, 1):
        where = [jax.random.randint(jax.random.fold_in(key, axis), (), 0, length) for axis, length in enumerate(values.shape)]
        where[longest] = (where[longest] + shift) % values.shape[longest]
        spots.append(tuple(where))
    return values.at[spots[0]].set(low).at[spots[1]].set(high)


def shard_levels(key, shape, cuts, low, high):
    def one(position, parts):
        steps = jax.random.uniform(jax.random.fold_in(jax.random.fold_in(key, 6), position), (parts,), jnp.float32, low / len(cuts), high / len(cuts))
        return jnp.repeat(jnp.exp(steps), shape[position] // parts).reshape((-1,) + (1,) * (len(shape) - position - 1))

    level = one(*cuts[0])
    for cut in cuts[1:]:
        level = level * one(*cut)
    return level


def centred(own_key, shape, scale, bound, cuts=(), held_as=jnp.bfloat16):
    array = scale * jax.random.normal(own_key, shape, jnp.float32)
    if cuts:
        array = array * shard_levels(own_key, shape, cuts, -0.22, 0.18)
    return jnp.clip(array, -bound, bound).astype(held_as)


def setup_inputs(seed: int = 0) -> dict:
    arg_keys = jax.random.split(jax.random.key(seed), 4)
    traces = centred(arg_keys[0], (SEGMENTS, FR, CHANNELS, NFFT), 1.0, 6.0, ((0, 4), (2, 64)))
    valid_flags = draw_valid_flags(jax.random.fold_in(arg_keys[3], 71), 0)
    source_block = touch_ends(jax.random.randint(arg_keys[2], (STEPS,), 0, CHANNELS // SB), jax.random.fold_in(arg_keys[2], 1), 0, (CHANNELS // SB) - 1).astype(jnp.int32)
    return dict(traces=traces, valid_flags=valid_flags, source_block=source_block)


def dft_table(length):
    times = jnp.arange(length, dtype=jnp.int32)
    bins = jnp.arange(length // 2, dtype=jnp.int32)
    phase = times[:, None] * bins[None, :] % length
    angle = phase.astype(jnp.float32) * (2.0 * math.pi / length)
    return jnp.concatenate([jnp.cos(angle), -jnp.sin(angle)], axis=1).astype(jnp.bfloat16)

def lag_table(length, count):
    bins = jnp.arange(length // 2, dtype=jnp.int32)
    shifts = jnp.arange(count, dtype=jnp.int32) - count // 2 + length
    phase = bins[:, None] * shifts[None, :] % length
    angle = phase.astype(jnp.float32) * (2.0 * math.pi / length)
    return jnp.concatenate([jnp.cos(angle), -jnp.sin(angle)], axis=0)

def whiten(spectrum):
    width = spectrum.shape[-1] // 2
    real_part = spectrum[..., :width]
    imag_part = spectrum[..., width:]
    power = real_part * real_part + imag_part * imag_part
    level = 0.25 * lax.optimization_barrier(jnp.mean(power, axis=-1, keepdims=True)) + 1e-06
    factor = 1.0 / jnp.sqrt(power + level)
    return (spectrum * jnp.concatenate([factor, factor], axis=-1)).astype(jnp.bfloat16)

def cross(sources, receivers):
    width = sources.shape[-1] // 2
    s_real = sources[..., :width].astype(jnp.float32)
    s_imag = sources[..., width:].astype(jnp.float32)
    r_real = receivers[..., :width].astype(jnp.float32)
    r_imag = receivers[..., width:].astype(jnp.float32)

    def contract(left, right):
        return jnp.einsum('sfjk,sfck->jck', left, right)
    real_sum = contract(s_real, r_real) + contract(s_imag, r_imag)
    imag_sum = contract(s_real, r_imag) - contract(s_imag, r_real)
    return jnp.concatenate([real_sum, imag_sum], axis=-1)

def reference(traces, valid_flags, source_block):
    table = dft_table(NFFT)
    lagtab = lag_table(NFFT, LAGS)

    def spectra(segment):
        flat = segment.reshape(-1, NFFT)
        return whiten(jnp.dot(flat, table, preferred_element_type=jnp.float32)).reshape(FR, CHANNELS, NFFT)
    whitened = lax.map(spectra, traces)
    masked = whitened * valid_flags.astype(jnp.bfloat16)[:, None, None, None]
    count = FR * jnp.sum(valid_flags)
    denom = jnp.sqrt(jnp.float32(NFFT // 2) * count.astype(jnp.float32))
    group_rcv = masked.reshape(N_SEG, S_DEV, FR, CHANNELS, NFFT)
    results = []
    for number in range(STEPS):
        start = (source_block[number] * SB).astype(jnp.int32)
        sources = lax.dynamic_slice_in_dim(whitened, start, SB, 2)
        group_src = sources.reshape(N_SEG, S_DEV, FR, SB, NFFT)

        def accumulate(total, pair):
            rounded = lax.optimization_barrier(cross(pair[0], pair[1]).astype(jnp.bfloat16))
            return (total + rounded.astype(jnp.float32), None)
        stack, _ = lax.scan(accumulate, jnp.zeros((SB, CHANNELS, NFFT), jnp.float32), (group_src, group_rcv))
        lagged = jnp.dot(stack.reshape(-1, NFFT), lagtab, precision=lax.Precision.HIGHEST, preferred_element_type=jnp.float32)
        results.append(lagged.reshape(SB, CHANNELS, LAGS) / denom)
    return jnp.stack(results)
```

```python
import math

import jax
import jax.numpy as jnp
import ml_dtypes
import numpy as np
from jax import lax
from jax.experimental import pallas as pl
from jax.experimental.pallas import tpu as pltpu
from jax.sharding import PartitionSpec as P

MESH = pl.DeviceIdType.MESH
NFFT = 2048
HALF = NFFT // 2
LAGS = 512
SB = 16
STEPS = 4
NY, NZ = 4, 8
KQ = 4
QB = HALF // KQ
QL = 2 * QB
F32, BF16 = jnp.float32, jnp.bfloat16


def dft_table():
    t = np.arange(NFFT)[:, None]
    k = np.arange(HALF)[None, :]
    angle = ((t * k) % NFFT) * (2.0 * math.pi / NFFT)
    both = np.stack([np.cos(angle), -np.sin(angle)], 1).reshape(NFFT, 2, KQ, QB)
    return both.transpose(2, 0, 1, 3).reshape(KQ, NFFT, QL).astype(ml_dtypes.bfloat16)


def lag_table():
    k = np.arange(HALF)[:, None]
    tau = np.arange(LAGS)[None, :] - LAGS // 2 + NFFT
    angle = ((k * tau) % NFFT) * (2.0 * math.pi / NFFT)
    full = np.concatenate([np.cos(angle), -np.sin(angle)], 0).astype(np.float32)
    high = full.astype(ml_dtypes.bfloat16)
    low = (full - high.astype(np.float32)).astype(ml_dtypes.bfloat16)
    parts = [a[:, h * 256 : h * 256 + 256] for a in (high, low) for h in (0, 1)]
    return np.stack(parts)


def kernel(
    x_ref, flags, blocks, tab_hbm, lag_hbm, out,
    tab, lag, spec, w, rb1, rp, cand, rb20, rb21, rb22, rb23, src, r3, s3, z, lf,
    send_c, recv_c, send_x, recv_x, send_h, recv_h, own_c, own_x, own_h,
    tab_sem, a1_s, a1_r, rx_sem, az_s, az_r, gz_s, gz_r, gy_s, gy_r, rs_s, rs_r,
):
    rb2 = (rb20, rb21, rb22, rb23)
    rcv, seg = lax.axis_index("rcv"), lax.axis_index("seg")
    px, py, pz = rcv // 32, (rcv // 8) % 4, rcv % 8
    ph, pc = seg // 2, seg % 2
    me_q = px * NY + py

    def at_xy(dx, dy):
        return (px + dx) % 2, (py + dy) % NY

    def dev_xy(dx, dy):
        tx, ty = at_xy(dx, dy)
        return (tx * 32 + ty * 8 + pz, seg)

    def dev_z(dz):
        return (px * 32 + py * 8 + (pz + dz) % NZ, seg)

    dev_c = (rcv, ph * 2 + 1 - pc)
    dev_h = (rcv, (1 - ph) * 2 + pc)
    plane = [(dx, dy) for dx in (0, 1) for dy in range(NY) if dx or dy]

    barrier = pltpu.get_barrier_semaphore()
    peers = [dev_xy(*d) for d in plane] + [dev_z(d) for d in range(1, NZ)] + [dev_c, dev_h]
    for peer in peers:
        pl.semaphore_signal(barrier, inc=1, device_id=peer, device_id_type=MESH)

    loads = [pltpu.make_async_copy(tab_hbm.at[q], tab.at[q], tab_sem.at[q]) for q in range(KQ)]
    loads.append(pltpu.make_async_copy(lag_hbm, lag, tab_sem.at[KQ]))
    for load in loads:
        load.start()

    def remote(a, b, s, r, peer):
        return pltpu.make_async_remote_copy(
            src_ref=a, dst_ref=b, send_sem=s, recv_sem=r, device_id=peer, device_id_type=MESH
        )

    rows = x_ref[...].reshape(256, NFFT)
    for q in range(KQ):
        loads[q].wait()
        spec[q] = jnp.dot(rows, tab[q], preferred_element_type=F32)

    def whiten(row, _):
        at = pl.ds(pl.multiple_of(row * SB, SB), SB)
        parts = [spec[q, at, :] for q in range(KQ)]
        powers = [p[:, :QB] * p[:, :QB] + p[:, QB:] * p[:, QB:] for p in parts]
        total = sum(jnp.sum(p, axis=-1, keepdims=True) for p in powers)
        level = 0.25 * (total * (1.0 / HALF)) + 1e-06
        for q in range(KQ):
            factor = lax.rsqrt(powers[q] + level)
            w[row // 8, q, row % 8] = (parts[q] * jnp.concatenate([factor, factor], -1)).astype(BF16)
        return 0

    lax.fori_loop(0, 16, whiten, 0)

    pl.semaphore_wait(barrier, len(peers))

    sent = []
    first = []
    for i, (dx, dy) in enumerate(plane):
        tx, ty = at_xy(dx, dy)
        copy = remote(w.at[tx, ty], rb1.at[me_q], a1_s.at[i], a1_r.at[i], dev_xy(dx, dy))
        copy.start()
        first.append(copy)
    swap = remote(w.at[1 - px], rp, rx_sem.at[0], rx_sem.at[1], dev_xy(1, 0))
    swap.start()
    sent += first + [swap]
    rb1[me_q] = w[px, py]

    def fill(ref, row):
        def one(f, _):
            for q in range(KQ):
                re = ref[q, f, :, :QB].astype(F32)
                im = ref[q, f, :, QB:].astype(F32)
                at = (f, pl.ds(pl.multiple_of(row * SB, SB), SB), pl.ds(q * QB, QB))
                r3[(0,) + at] = re
                r3[(1,) + at] = im
                r3[(2,) + at] = re + im
            return 0

        lax.fori_loop(0, NZ, one, 0)

    fill(w.at[px], px)
    for copy in first:
        copy.wait_recv()
    across = []
    for s in range(STEPS):
        chosen = rb1[blocks[s] // NZ]
        cand[:, s] = chosen
        rb2[s][pz] = cand[pz, s]
        group = []
        for dz in range(1, NZ):
            copy = remote(cand.at[(pz + dz) % NZ, s], rb2[s].at[pz], az_s.at[s, dz], az_r.at[s, dz], dev_z(dz))
            copy.start()
            group.append(copy)
        across.append(group)
        sent += group
    along = []
    for s in range(STEPS):
        for copy in across[s]:
            copy.wait_recv()
        src[s, py, pz] = rb2[s][blocks[s] % NZ]
        group = []
        for dz in range(1, NZ):
            here = src.at[s, py, pz]
            copy = remote(here, here, gz_s.at[s, dz], gz_r.at[s, dz], dev_z(dz))
            copy.start()
            group.append(copy)
        along.append(group)
        sent += group
    over = []
    for s in range(STEPS):
        for copy in along[s]:
            copy.wait_recv()
        group = []
        for dy in (1, 3, 2):
            here = src.at[s, py]
            copy = remote(here, here, gy_s.at[s, dy], gy_r.at[s, dy], dev_xy(0, dy))
            copy.start()
            group.append(copy)
        over.append(group)
        sent += group
    swap.wait_recv()
    fill(rp, 1 - px)
    loads[KQ].wait()

    count = flags[0]
    for g in range(1, 8):
        count = count + flags[g]
    scale = 1.0 / jnp.sqrt(jnp.full((SB, LAGS), HALF, F32) * (8 * count).astype(F32))
    keep = flags[seg * 2 + px].astype(F32)

    stage_c, stage_x, stage_h = [], [], []

    def to_x(s):
        stage_c[s].wait_recv()

        def one(b, _):
            for xc in range(2):
                own_c[b, xc] = own_c[b, xc] + recv_c[s, b // 4, b % 4, xc].astype(F32)
            send_x[s, b // 4, b % 4] = own_c[b, 1 - px].astype(BF16)
            own_x[s, b // 4, b % 4] = own_c[b, px]
            return 0

        lax.fori_loop(0, 8, one, 0)
        copy = remote(send_x.at[s], recv_x.at[s], rs_s.at[1, s], rs_r.at[1, s], dev_xy(1, 0))
        copy.start()
        stage_x.append(copy)
        sent.append(copy)

    def to_h(s):
        stage_x[s].wait_recv()
        for jj in range(4):
            send_h[s, jj] = (own_x[s, 1 - ph, jj] + recv_x[s, 1 - ph, jj].astype(F32)).astype(BF16)
            own_h[s, jj] = own_x[s, ph, jj] + recv_x[s, ph, jj].astype(F32)
        copy = remote(send_h.at[s], recv_h.at[s], rs_s.at[2, s], rs_r.at[2, s], dev_h)
        copy.start()
        stage_h.append(copy)
        sent.append(copy)

    def finish(s):
        stage_h[s].wait_recv()
        for jj in range(4):
            out[s, jj] = (own_h[s, jj] + recv_h[s, jj].astype(F32)) * scale

    for s in range(STEPS):
        for copy in over[s]:
            copy.wait_recv()

        def split(f, _, s=s):
            for q in range(KQ):
                re = src[s, q, f, :, :QB].astype(F32)
                im = src[s, q, f, :, QB:].astype(F32)
                at = (f, slice(None), pl.ds(q * QB, QB))
                s3[(0,) + at] = re
                s3[(1,) + at] = im
                s3[(2,) + at] = re - im
            return 0

        lax.fori_loop(0, NZ, split, 0)

        def cross(kt, _):
            at = pl.ds(pl.multiple_of(kt * 128, 128), 128)
            im_at = pl.ds(pl.multiple_of(HALF + kt * 128, 128), 128)
            for first_j in range(0, SB, 2):
                sums = [[jnp.zeros((2 * SB, 128), F32) for _ in range(3)] for _ in range(2)]
                for f in range(NZ):
                    r = [r3[c, f, :, at] for c in range(3)]
                    for n in range(2):
                        j = first_j + n
                        for c in range(3):
                            sums[n][c] = sums[n][c] + s3[c, f, j : j + 1, at] * r[c]
                for n in range(2):
                    j = first_j + n
                    a, b, c = sums[n]
                    row = ((j // 4) % 2 * 2 + j // 8) * 4 + j % 4
                    z[row * 32 : row * 32 + 32, at] = (a + b).astype(BF16)
                    z[row * 32 : row * 32 + 32, im_at] = (c - a + b).astype(BF16)
            return 0

        lax.fori_loop(0, HALF // 128, cross, 0)

        def to_lags(n, _):
            both = jnp.dot(z[...], lag[n], preferred_element_type=F32)
            both = both + jnp.dot(z[...], lag[n + 2], preferred_element_type=F32)
            both = both * keep
            lf[:, :, :, :, pl.ds(pl.multiple_of(n * 256, 256), 256)] = both.reshape(2, 8, 2, SB, 256)
            return 0

        lax.fori_loop(0, 2, to_lags, 0)
        if s >= 1:
            to_x(s - 1)

        def part(b, _, s=s):
            for xc in range(2):
                send_c[s, b // 4, b % 4, xc] = lf[1 - pc, b, xc].astype(BF16)
                own_c[b, xc] = lf[pc, b, xc]
            return 0

        lax.fori_loop(0, 8, part, 0)
        copy = remote(send_c.at[s], recv_c.at[s], rs_s.at[0, s], rs_r.at[0, s], dev_c)
        copy.start()
        stage_c.append(copy)
        sent.append(copy)
        if s >= 2:
            to_h(s - 2)
        if s >= 3:
            finish(s - 3)
    last = STEPS - 1
    to_x(last)
    to_h(last - 1)
    finish(last - 2)
    to_h(last)
    finish(last - 1)
    finish(last)
    for copy in sent:
        copy.wait_send()


def local(traces, valid_flags, source_block):
    vmem = lambda *shape, dtype=BF16: pltpu.VMEM(shape, dtype)
    dma = lambda *shape: pltpu.SemaphoreType.DMA(shape)
    return pl.pallas_call(
        kernel,
        out_shape=jax.ShapeDtypeStruct((STEPS, 4, SB, LAGS), F32),
        in_specs=[
            pl.BlockSpec(memory_space=pltpu.VMEM),
            pl.BlockSpec(memory_space=pltpu.SMEM),
            pl.BlockSpec(memory_space=pltpu.SMEM),
            pl.BlockSpec(memory_space=pl.ANY),
            pl.BlockSpec(memory_space=pl.ANY),
        ],
        out_specs=pl.BlockSpec(memory_space=pltpu.VMEM),
        scratch_shapes=[
            vmem(KQ, NFFT, QL),
            vmem(4, NFFT, LAGS // 2),
            vmem(KQ, 256, QL, dtype=F32),
            vmem(2, KQ, NZ, SB, QL),
            vmem(2 * NY, NZ, SB, QL),
            vmem(KQ, NZ, SB, QL),
            vmem(NZ, STEPS, SB, QL),
            *[vmem(NZ, SB, QL) for _ in range(STEPS)],
            vmem(STEPS, KQ, NZ, SB, QL),
            vmem(3, NZ, 2 * SB, HALF, dtype=F32),
            vmem(3, NZ, SB, HALF, dtype=F32),
            vmem(2 * SB * SB, NFFT),
            vmem(2, 8, 2, SB, LAGS, dtype=F32),
            vmem(STEPS, 2, 4, 2, SB, LAGS),
            vmem(STEPS, 2, 4, 2, SB, LAGS),
            vmem(STEPS, 2, 4, SB, LAGS),
            vmem(STEPS, 2, 4, SB, LAGS),
            vmem(STEPS, 4, SB, LAGS),
            vmem(STEPS, 4, SB, LAGS),
            vmem(8, 2, SB, LAGS, dtype=F32),
            vmem(STEPS, 2, 4, SB, LAGS, dtype=F32),
            vmem(STEPS, 4, SB, LAGS, dtype=F32),
            dma(KQ + 1),
            dma(7), dma(7), dma(2),
            dma(STEPS, NZ), dma(STEPS, NZ),
            dma(STEPS, NZ), dma(STEPS, NZ),
            dma(STEPS, NY), dma(STEPS, NY),
            dma(3, STEPS), dma(3, STEPS),
        ],
        compiler_params=pltpu.CompilerParams(
            collective_id=0, has_side_effects=True, vmem_limit_bytes=56 * 2**20
        ),
        name="correlate",
    )(traces, valid_flags, source_block, jnp.asarray(dft_table()), jnp.asarray(lag_table()))


def solution(mesh):
    placed = (P("seg", None, "rcv", None), P(), P())
    return jax.shard_map(
        local, mesh=mesh, in_specs=placed, out_specs=P(None, "seg", "rcv", None), check_vma=False
    )
```

```python
import math

import jax
import jax.numpy as jnp
import ml_dtypes
import numpy as np
from jax import lax
from jax.experimental import pallas as pl
from jax.experimental.pallas import tpu as pltpu
from jax.sharding import PartitionSpec as P

MESH = pl.DeviceIdType.MESH
NFFT = 2048
HALF = NFFT // 2
LAGS = 512
SB = 16
STEPS = 4
NY, NZ = 4, 8
KQ = 4
PB = HALF // KQ // 2
PL = 2 * PB
QL = 2 * PL
GROUPS = [(0, 0, 2), (0, 2, 2), (1, 0, 1), (1, 1, 1), (1, 2, 1), (1, 3, 1)]
F32, BF16 = jnp.float32, jnp.bfloat16


def dft_table():
    t = np.arange(NFFT)[:, None]
    k = np.arange(HALF)[None, :]
    angle = ((t * k) % NFFT) * (2.0 * math.pi / NFFT)
    both = np.stack([np.cos(angle), -np.sin(angle)], 1).reshape(NFFT, 2, KQ, 2, PB)
    return both.transpose(2, 0, 3, 1, 4).reshape(KQ, NFFT, QL).astype(ml_dtypes.bfloat16)


def lag_table():
    k = np.arange(HALF)[:, None]
    tau = np.arange(LAGS)[None, :] - LAGS // 2 + NFFT
    angle = ((k * tau) % NFFT) * (2.0 * math.pi / NFFT)
    full = np.stack([np.cos(angle), -np.sin(angle)], 0).reshape(2, 2 * KQ, PB, LAGS)
    return full.transpose(1, 0, 2, 3).reshape(NFFT, LAGS).astype(ml_dtypes.bfloat16)


def kernel(
    x_ref, flags, blocks, tab_hbm, lag_hbm, out,
    tab, lag, spec, w, rb1a, rb1b, rp, cand, rb20, rb21, rb22, rb23, rb24, rb25, src, r3, s3, z,
    send_c, recv_c, send_d, recv_d, own_c, own_d,
    tab_sem, a1_s, a1_r, rx_sem, az_s, az_r, gz_s, gz_r, gy_s, gy_r, rs_s, rs_r,
):
    rb1 = (rb1a, rb1b)
    rb2 = (rb20, rb21, rb22, rb23, rb24, rb25)
    rcv, seg = lax.axis_index("rcv"), lax.axis_index("seg")
    px, py, pz = rcv // 32, (rcv // 8) % 4, rcv % 8
    ph, pc = seg // 2, seg % 2
    me_q = px * NY + py

    def at_xy(dx, dy):
        return (px + dx) % 2, (py + dy) % NY

    def dev_xy(dx, dy):
        tx, ty = at_xy(dx, dy)
        return (tx * 32 + ty * 8 + pz, seg)

    def dev_z(dz):
        return (px * 32 + py * 8 + (pz + dz) % NZ, seg)

    dev_c = (rcv, ph * 2 + 1 - pc)

    def dev_far(dh, dx):
        return (((px + dx) % 2) * 32 + py * 8 + pz, ((ph + dh) % 2) * 2 + pc)

    plane = [(dx, dy) for dx in (0, 1) for dy in range(NY) if dx or dy]

    barrier = pltpu.get_barrier_semaphore()
    peers = [dev_xy(*d) for d in plane] + [dev_z(d) for d in range(1, NZ)] + [dev_c, dev_far(1, 0), dev_far(1, 1)]
    for peer in peers:
        pl.semaphore_signal(barrier, inc=1, device_id=peer, device_id_type=MESH)

    loads = [pltpu.make_async_copy(tab_hbm.at[q], tab.at[q], tab_sem.at[q]) for q in range(KQ)]
    loads.append(pltpu.make_async_copy(lag_hbm, lag, tab_sem.at[KQ]))
    for load in loads[:KQ]:
        load.start()

    def remote(a, b, s, r, peer):
        return pltpu.make_async_remote_copy(
            src_ref=a, dst_ref=b, send_sem=s, recv_sem=r, device_id=peer, device_id_type=MESH
        )

    rows = x_ref[...].reshape(256, NFFT)
    for q in range(KQ):
        loads[q].wait()
        spec[q] = jnp.dot(rows, tab[q], preferred_element_type=F32)

    loads[KQ].start()

    def whiten(row, _):
        at = pl.ds(pl.multiple_of(row * SB, SB), SB)
        parts = [spec[q, at, h * PL : h * PL + PL] for q in range(KQ) for h in range(2)]
        powers = [p[:, :PB] * p[:, :PB] + p[:, PB:] * p[:, PB:] for p in parts]
        total = jnp.sum(sum(powers), axis=-1, keepdims=True)
        level = 0.25 * (total * (1.0 / HALF)) + 1e-06
        for i, (part, power) in enumerate(zip(parts, powers)):
            factor = lax.rsqrt(power + level)
            w[row // 8, i % 2, i // 2, row % 8] = (part * jnp.concatenate([factor, factor], -1)).astype(BF16)
        return 0

    lax.fori_loop(0, 16, whiten, 0)

    pl.semaphore_wait(barrier, len(peers))

    sent = []
    first = [[], []]
    for h in range(2):
        for i, (dx, dy) in enumerate(plane):
            tx, ty = at_xy(dx, dy)
            first[h].append(
                remote(w.at[tx, h, ty], rb1[h].at[me_q], a1_s.at[h, i], a1_r.at[h, i], dev_xy(dx, dy))
            )
    swap = remote(w.at[1 - px], rp, rx_sem.at[0], rx_sem.at[1], dev_xy(1, 0))

    def fill(ref, row):
        def one(f, _):
            for q in range(KQ):
                for h in range(2):
                    re = ref[h, q, f, :, :PB].astype(F32)
                    im = ref[h, q, f, :, PB:].astype(F32)
                    lanes = pl.ds((q * 2 + h) * PB, PB)
                    at = (f, pl.ds(pl.multiple_of(row * SB, SB), SB), lanes)
                    r3[(0,) + at] = re
                    r3[(1,) + at] = im
                    r3[(2,) + at] = re + im
            return 0

        lax.fori_loop(0, NZ, one, 0)

    def choose(h):
        rb1[h][me_q] = w[px, h, py]
        for copy in first[h]:
            copy.wait_recv()
        for s in range(STEPS):
            cand[h, :, s] = rb1[h][blocks[s] // NZ]

    across, along, over = {}, {}, {}

    def send_across(g):
        h, s0, n = GROUPS[g]
        rb2[g][pz] = cand[h, pz, s0 : s0 + n]
        across[g] = []
        for dz in range(1, NZ):
            here = cand.at[h, (pz + dz) % NZ, pl.ds(s0, n)]
            copy = remote(here, rb2[g].at[pz], az_s.at[g, dz], az_r.at[g, dz], dev_z(dz))
            copy.start()
            across[g].append(copy)
        sent.extend(across[g])

    def send_along(g):
        h, s0, n = GROUPS[g]
        for copy in across[g]:
            copy.wait_recv()
        for i in range(n):
            src[h, s0 + i, py, pz] = rb2[g][blocks[s0 + i] % NZ, i]
        along[g] = []
        here = src.at[h, pl.ds(s0, n), py, pz]
        for dz in range(1, NZ):
            copy = remote(here, here, gz_s.at[g, dz], gz_r.at[g, dz], dev_z(dz))
            copy.start()
            along[g].append(copy)
        sent.extend(along[g])

    def send_over(g):
        h, s0, n = GROUPS[g]
        for copy in along[g]:
            copy.wait_recv()
        over[g] = []
        here = src.at[h, pl.ds(s0, n), py]
        for dy in (1, 3, 2):
            copy = remote(here, here, gy_s.at[g, dy], gy_r.at[g, dy], dev_xy(0, dy))
            copy.start()
            over[g].append(copy)
        sent.extend(over[g])

    def unit(h, s, q):
        def split(f, _):
            re = src[h, s, q, f, :, :PB].astype(F32)
            im = src[h, s, q, f, :, PB:].astype(F32)
            s3[0, f] = re
            s3[1, f] = im
            s3[2, f] = re - im
            return 0

        lax.fori_loop(0, NZ, split, 0)
        at = pl.ds(pl.multiple_of((q * 2 + h) * PB, PB), PB)
        re_at = pl.ds(pl.multiple_of((q * 2 + h) * PL, PL), PB)
        im_at = pl.ds(pl.multiple_of((q * 2 + h) * PL + PB, PB), PB)
        for xc in range(2):
            for first_j in range(0, SB, 4):
                sums = [[None] * 3 for _ in range(4)]
                for f in range(NZ):
                    for c in range(3):
                        r = r3[c, f, xc * SB : xc * SB + SB, at]
                        for n in range(4):
                            j = first_j + n
                            term = s3[c, f, j : j + 1, :] * r
                            sums[n][c] = term if f == 0 else sums[n][c] + term
                for n in range(4):
                    j = first_j + n
                    a, b, c = sums[n]
                    row = (((j // 4) % 2 * 2 + j // 8) * 4 + j % 4) * 32 + xc * SB
                    z[s, row : row + SB, re_at] = (a + b).astype(BF16)
                    z[s, row : row + SB, im_at] = (c - a + b).astype(BF16)

    def own_units(h, s0, n):
        def one(i, _):
            unit(h, s0 + i, py)
            return 0

        lax.fori_loop(0, n, one, 0)

    def other_units(g):
        h, s0, n = GROUPS[g]
        for copy in over[g]:
            copy.wait_recv()

        def one(i, _):
            unit(h, s0 + i // 3, (py + 1 + i % 3) % NY)
            return 0

        lax.fori_loop(0, 3 * n, one, 0)

    for copy in first[0]:
        copy.start()
    fill(w.at[px], px)
    for copy in first[0]:
        copy.wait_send()
    for copy in first[1]:
        copy.start()
    sent += first[1]
    choose(0)
    send_across(0)
    send_across(1)
    choose(1)
    swap.start()
    sent.append(swap)
    send_along(0)
    send_along(1)
    for g in range(2, 6):
        send_across(g)
    send_over(0)
    send_over(1)
    for g in range(2, 6):
        send_along(g)
    swap.wait_recv()
    fill(rp, 1 - px)
    own_units(0, 0, STEPS)
    for g in range(2, 6):
        send_over(g)
        own_units(1, g - 2, 1)
    loads[KQ].wait()

    count = flags[0]
    for g in range(1, 8):
        count = count + flags[g]
    scale = 1.0 / jnp.sqrt(jnp.full((SB, LAGS), HALF, F32) * (8 * count).astype(F32))
    keep = flags[seg * 2 + px].astype(F32)

    stage_c, stage_d = [], []
    others = [(0, 1), (1, 0), (1, 1)]

    def to_chips(s):
        stage_c[s].wait_recv()

        def one(b, _):
            for xc in range(2):
                both = own_c[s, b, xc] + recv_c[s, b // 4, b % 4, xc].astype(F32)
                own_d[s, b // 4, xc, b % 4] = both
                send_d[s, b // 4, xc, b % 4] = both.astype(BF16)
            return 0

        lax.fori_loop(0, 8, one, 0)
        group = []
        for i, (dh, dx) in enumerate(others):
            copy = remote(
                send_d.at[s, (ph + dh) % 2, (px + dx) % 2], recv_d.at[s, i],
                rs_s.at[1 + i, s], rs_r.at[1 + i, s], dev_far(dh, dx),
            )
            copy.start()
            group.append(copy)
        stage_d.append(group)
        sent.extend(group)

    def finish(s):
        for copy in stage_d[s]:
            copy.wait_recv()
        for jj in range(4):
            total = own_d[s, ph, px, jj]
            for i in range(3):
                total = total + recv_d[s, i, jj].astype(F32)
            out[s, jj] = total * scale

    for s in range(STEPS):
        if s == 0:
            other_units(0)
            other_units(1)
        other_units(2 + s)
        for own in (False, True):
            half = pc if own else 1 - pc
            rows = z[s, pl.ds(pl.multiple_of(half * 256, 256), 256), :]
            lags = jnp.dot(rows, lag[...], preferred_element_type=F32) * keep
            if own:
                own_c[s] = lags.reshape(8, 2, SB, LAGS)
            else:
                send_c[s] = lags.astype(BF16).reshape(2, 4, 2, SB, LAGS)
                copy = remote(send_c.at[s], recv_c.at[s], rs_s.at[0, s], rs_r.at[0, s], dev_c)
                copy.start()
                stage_c.append(copy)
                sent.append(copy)
        if s >= 1:
            to_chips(s - 1)

        if s >= 2:
            finish(s - 2)
    last = STEPS - 1
    to_chips(last)
    finish(last - 1)
    finish(last)
    for copy in sent:
        copy.wait_send()


def local(traces, valid_flags, source_block):
    vmem = lambda *shape, dtype=BF16: pltpu.VMEM(shape, dtype)
    dma = lambda *shape: pltpu.SemaphoreType.DMA(shape)
    return pl.pallas_call(
        kernel,
        out_shape=jax.ShapeDtypeStruct((STEPS, 4, SB, LAGS), F32),
        in_specs=[
            pl.BlockSpec(memory_space=pltpu.VMEM),
            pl.BlockSpec(memory_space=pltpu.SMEM),
            pl.BlockSpec(memory_space=pltpu.SMEM),
            pl.BlockSpec(memory_space=pl.ANY),
            pl.BlockSpec(memory_space=pl.ANY),
        ],
        out_specs=pl.BlockSpec(memory_space=pltpu.VMEM),
        scratch_shapes=[
            vmem(KQ, NFFT, QL),
            vmem(NFFT, LAGS),
            vmem(KQ, 256, QL, dtype=F32),
            vmem(2, 2, KQ, NZ, SB, PL),
            vmem(2 * NY, NZ, SB, PL),
            vmem(2 * NY, NZ, SB, PL),
            vmem(2, KQ, NZ, SB, PL),
            vmem(2, NZ, STEPS, SB, PL),
            *[vmem(NZ, n, SB, PL) for _, _, n in GROUPS],
            vmem(2, STEPS, KQ, NZ, SB, PL),
            vmem(3, NZ, 2 * SB, HALF, dtype=F32),
            vmem(3, NZ, SB, PB, dtype=F32),
            vmem(STEPS, 2 * SB * SB, NFFT),
            vmem(STEPS, 2, 4, 2, SB, LAGS),
            vmem(STEPS, 2, 4, 2, SB, LAGS),
            vmem(STEPS, 2, 2, 4, SB, LAGS),
            vmem(STEPS, 3, 4, SB, LAGS),
            vmem(STEPS, 8, 2, SB, LAGS, dtype=F32),
            vmem(STEPS, 2, 2, 4, SB, LAGS, dtype=F32),
            dma(KQ + 1),
            dma(2, 7), dma(2, 7), dma(2),
            dma(6, NZ), dma(6, NZ),
            dma(6, NZ), dma(6, NZ),
            dma(6, NY), dma(6, NY),
            dma(4, STEPS), dma(4, STEPS),
        ],
        compiler_params=pltpu.CompilerParams(
            collective_id=0, has_side_effects=True, vmem_limit_bytes=56 * 2**20
        ),
        name="correlate",
    )(traces, valid_flags, source_block, jnp.asarray(dft_table()), jnp.asarray(lag_table()))


def solution(mesh):
    placed = (P("seg", None, "rcv", None), P(), P())
    return jax.shard_map(
        local, mesh=mesh, in_specs=placed, out_specs=P(None, "seg", "rcv", None), check_vma=False
    )
```

```python
import math

import jax
import jax.numpy as jnp
import ml_dtypes
import numpy as np
from jax import lax
from jax.experimental import pallas as pl
from jax.experimental.pallas import tpu as pltpu
from jax.sharding import PartitionSpec as P

MESH = pl.DeviceIdType.MESH
NFFT = 2048
HALF = NFFT // 2
LAGS = 512
SB = 16
STEPS = 4
NY, NZ = 4, 8
KQ = 4
PB = HALF // KQ // 2
PL = 2 * PB
QL = 2 * PL
GROUPS = [(0, 0, 2), (0, 2, 2), (1, 0, 1), (1, 1, 1), (1, 2, 1), (1, 3, 1)]
F32, BF16 = jnp.float32, jnp.bfloat16


def dft_table():
    t = np.arange(NFFT)[:, None]
    k = np.arange(HALF)[None, :]
    angle = ((t * k) % NFFT) * (2.0 * math.pi / NFFT)
    both = np.stack([np.cos(angle), -np.sin(angle)], 1).reshape(NFFT, 2, KQ, 2, PB)
    return both.transpose(2, 0, 3, 1, 4).reshape(KQ, NFFT, QL).astype(ml_dtypes.bfloat16)


def lag_table():
    k = np.arange(HALF)[:, None]
    tau = np.arange(LAGS)[None, :] - LAGS // 2 + NFFT
    angle = ((k * tau) % NFFT) * (2.0 * math.pi / NFFT)
    full = np.stack([np.cos(angle), -np.sin(angle)], 0).reshape(2, 2 * KQ, PB, LAGS)
    return full.transpose(1, 0, 2, 3).reshape(NFFT, LAGS).astype(ml_dtypes.bfloat16)


def kernel(
    x_ref, flags, blocks, tab_hbm, lag_hbm, out,
    tab, lag, spec, w, rb1a, rb1b, rp, cand, rb20, rb21, rb22, rb23, rb24, rb25, src, r3, s3, z, lf,
    send_c, recv_c, send_d, recv_d, own_c, own_d,
    tab_sem, a1_s, a1_r, rx_sem, az_s, az_r, gz_s, gz_r, gy_s, gy_r, rs_s, rs_r,
):
    rb1 = (rb1a, rb1b)
    rb2 = (rb20, rb21, rb22, rb23, rb24, rb25)
    rcv, seg = lax.axis_index("rcv"), lax.axis_index("seg")
    px, py, pz = rcv // 32, (rcv // 8) % 4, rcv % 8
    ph, pc = seg // 2, seg % 2
    me_q = px * NY + py

    def at_xy(dx, dy):
        return (px + dx) % 2, (py + dy) % NY

    def dev_xy(dx, dy):
        tx, ty = at_xy(dx, dy)
        return (tx * 32 + ty * 8 + pz, seg)

    def dev_z(dz):
        return (px * 32 + py * 8 + (pz + dz) % NZ, seg)

    dev_c = (rcv, ph * 2 + 1 - pc)

    def dev_far(dh, dx):
        return (((px + dx) % 2) * 32 + py * 8 + pz, ((ph + dh) % 2) * 2 + pc)

    plane = [(dx, dy) for dx in (0, 1) for dy in range(NY) if dx or dy]

    barrier = pltpu.get_barrier_semaphore()
    peers = [dev_xy(*d) for d in plane] + [dev_z(d) for d in range(1, NZ)] + [dev_c, dev_far(1, 0), dev_far(1, 1)]
    for peer in peers:
        pl.semaphore_signal(barrier, inc=1, device_id=peer, device_id_type=MESH)

    loads = [pltpu.make_async_copy(tab_hbm.at[q], tab.at[q], tab_sem.at[q]) for q in range(KQ)]
    loads.append(pltpu.make_async_copy(lag_hbm, lag, tab_sem.at[KQ]))
    for load in loads[:KQ]:
        load.start()

    def remote(a, b, s, r, peer):
        return pltpu.make_async_remote_copy(
            src_ref=a, dst_ref=b, send_sem=s, recv_sem=r, device_id=peer, device_id_type=MESH
        )

    rows = x_ref[...].reshape(256, NFFT)
    for q in range(KQ):
        loads[q].wait()
        spec[q] = jnp.dot(rows, tab[q], preferred_element_type=F32)

    loads[KQ].start()

    def whiten(row, _):
        at = pl.ds(pl.multiple_of(row * SB, SB), SB)
        parts = [spec[q, at, h * PL : h * PL + PL] for q in range(KQ) for h in range(2)]
        powers = [p[:, :PB] * p[:, :PB] + p[:, PB:] * p[:, PB:] for p in parts]
        total = jnp.sum(sum(powers), axis=-1, keepdims=True)
        level = 0.25 * (total * (1.0 / HALF)) + 1e-06
        for i, (part, power) in enumerate(zip(parts, powers)):
            factor = lax.rsqrt(power + level)
            w[row // 8, i % 2, i // 2, row % 8] = (part * jnp.concatenate([factor, factor], -1)).astype(BF16)
        return 0

    lax.fori_loop(0, 16, whiten, 0)

    pl.semaphore_wait(barrier, len(peers))

    sent = []
    first = [[], []]
    for h in range(2):
        for i, (dx, dy) in enumerate(plane):
            tx, ty = at_xy(dx, dy)
            first[h].append(
                remote(w.at[tx, h, ty], rb1[h].at[me_q], a1_s.at[h, i], a1_r.at[h, i], dev_xy(dx, dy))
            )
    swap = remote(w.at[1 - px], rp, rx_sem.at[0], rx_sem.at[1], dev_xy(1, 0))

    def fill(ref, row):
        def one(f, _):
            for q in range(KQ):
                for h in range(2):
                    re = ref[h, q, f, :, :PB].astype(F32)
                    im = ref[h, q, f, :, PB:].astype(F32)
                    lanes = pl.ds((q * 2 + h) * PB, PB)
                    at = (f, pl.ds(pl.multiple_of(row * SB, SB), SB), lanes)
                    r3[(0,) + at] = re
                    r3[(1,) + at] = im
                    r3[(2,) + at] = re + im
            return 0

        lax.fori_loop(0, NZ, one, 0)

    def choose(h):
        rb1[h][me_q] = w[px, h, py]
        for copy in first[h]:
            copy.wait_recv()
        for s in range(STEPS):
            cand[h, :, s] = rb1[h][blocks[s] // NZ]

    across, along, over = {}, {}, {}

    def send_across(g):
        h, s0, n = GROUPS[g]
        rb2[g][pz] = cand[h, pz, s0 : s0 + n]
        across[g] = []
        for dz in range(1, NZ):
            here = cand.at[h, (pz + dz) % NZ, pl.ds(s0, n)]
            copy = remote(here, rb2[g].at[pz], az_s.at[g, dz], az_r.at[g, dz], dev_z(dz))
            copy.start()
            across[g].append(copy)
        sent.extend(across[g])

    def send_along(g):
        h, s0, n = GROUPS[g]
        for copy in across[g]:
            copy.wait_recv()
        for i in range(n):
            src[h, s0 + i, py, pz] = rb2[g][blocks[s0 + i] % NZ, i]
        along[g] = []
        here = src.at[h, pl.ds(s0, n), py, pz]
        for dz in range(1, NZ):
            copy = remote(here, here, gz_s.at[g, dz], gz_r.at[g, dz], dev_z(dz))
            copy.start()
            along[g].append(copy)
        sent.extend(along[g])

    def send_over(g):
        h, s0, n = GROUPS[g]
        for copy in along[g]:
            copy.wait_recv()
        over[g] = []
        here = src.at[h, pl.ds(s0, n), py]
        for dy in (1, 3, 2):
            copy = remote(here, here, gy_s.at[g, dy], gy_r.at[g, dy], dev_xy(0, dy))
            copy.start()
            over[g].append(copy)
        sent.extend(over[g])

    def unit(h, s, q):
        def split(f, _):
            re = src[h, s, q, f, :, :PB].astype(F32)
            im = src[h, s, q, f, :, PB:].astype(F32)
            s3[0, f] = re
            s3[1, f] = im
            s3[2, f] = re - im
            return 0

        lax.fori_loop(0, NZ, split, 0)
        at = pl.ds(pl.multiple_of((q * 2 + h) * PB, PB), PB)
        re_at = pl.ds(pl.multiple_of((q * 2 + h) * PL, PL), PB)
        im_at = pl.ds(pl.multiple_of((q * 2 + h) * PL + PB, PB), PB)
        for xc in range(2):
            for first_j in range(0, SB, 4):
                sums = [[None] * 3 for _ in range(4)]
                for f in range(NZ):
                    for c in range(3):
                        r = r3[c, f, xc * SB : xc * SB + SB, at]
                        for n in range(4):
                            j = first_j + n
                            term = s3[c, f, j : j + 1, :] * r
                            sums[n][c] = term if f == 0 else sums[n][c] + term
                for n in range(4):
                    j = first_j + n
                    a, b, c = sums[n]
                    row = (((j // 4) % 2 * 2 + j // 8) * 4 + j % 4) * 32 + xc * SB
                    z[s, row : row + SB, re_at] = (a + b).astype(BF16)
                    z[s, row : row + SB, im_at] = (c - a + b).astype(BF16)

    def own_units(h, s0, n):
        def one(i, _):
            unit(h, s0 + i, py)
            return 0

        lax.fori_loop(0, n, one, 0)

    def other_units(g):
        h, s0, n = GROUPS[g]
        for copy in over[g]:
            copy.wait_recv()

        def one(i, _):
            unit(h, s0 + i // 3, (py + 1 + i % 3) % NY)
            return 0

        lax.fori_loop(0, 3 * n, one, 0)

    for copy in first[0]:
        copy.start()
    fill(w.at[px], px)
    for copy in first[0]:
        copy.wait_send()
    for copy in first[1]:
        copy.start()
    choose(0)
    send_across(0)
    send_across(1)
    for copy in first[1]:
        copy.wait_send()
    swap.start()
    sent.append(swap)
    choose(1)
    send_along(0)
    send_along(1)
    for g in range(2, 6):
        send_across(g)
    send_over(0)
    send_over(1)
    swap.wait_recv()
    fill(rp, 1 - px)
    own_units(0, 0, STEPS)
    for g in range(2, 6):
        send_along(g)
    other_units(0)
    for g in range(2, 6):
        if g == 4:
            other_units(1)
        send_over(g)
        own_units(1, g - 2, 1)
    loads[KQ].wait()

    count = flags[0]
    for g in range(1, 8):
        count = count + flags[g]
    scale = 1.0 / jnp.sqrt(jnp.full((SB, LAGS), HALF, F32) * (8 * count).astype(F32))
    keep = flags[seg * 2 + px].astype(F32)

    stage_c, stage_d = [], []
    others = [(0, 1), (1, 0), (1, 1)]

    def to_chips(s):
        stage_c[s].wait_recv()

        def one(b, _):
            for xc in range(2):
                both = own_c[s, b, xc] + recv_c[s, b // 4, b % 4, xc].astype(F32)
                own_d[s, b // 4, xc, b % 4] = both
                send_d[s, b // 4, xc, b % 4] = both.astype(BF16)
            return 0

        lax.fori_loop(0, 8, one, 0)
        group = []
        for i, (dh, dx) in enumerate(others):
            copy = remote(
                send_d.at[s, (ph + dh) % 2, (px + dx) % 2], recv_d.at[s, i],
                rs_s.at[1 + i, s], rs_r.at[1 + i, s], dev_far(dh, dx),
            )
            copy.start()
            group.append(copy)
        stage_d.append(group)
        sent.extend(group)

    def finish(s):
        for copy in stage_d[s]:
            copy.wait_recv()
        for jj in range(4):
            total = own_d[s, ph, px, jj]
            for i in range(3):
                total = total + recv_d[s, i, jj].astype(F32)
            out[s, jj] = total * scale

    for s in range(STEPS):
        other_units(2 + s)
        lags = jnp.dot(z[s], lag[...], preferred_element_type=F32) * keep
        lf[...] = lags.reshape(2, 8, 2, SB, LAGS)
        send_c[s] = lf[1 - pc].astype(BF16).reshape(2, 4, 2, SB, LAGS)
        copy = remote(send_c.at[s], recv_c.at[s], rs_s.at[0, s], rs_r.at[0, s], dev_c)
        copy.start()
        stage_c.append(copy)
        sent.append(copy)
        own_c[s] = lf[pc]
        if s >= 1:
            to_chips(s - 1)

        if s >= 2:
            finish(s - 2)
    last = STEPS - 1
    to_chips(last)
    finish(last - 1)
    finish(last)
    for copy in sent:
        copy.wait_send()


def local(traces, valid_flags, source_block):
    vmem = lambda *shape, dtype=BF16: pltpu.VMEM(shape, dtype)
    dma = lambda *shape: pltpu.SemaphoreType.DMA(shape)
    return pl.pallas_call(
        kernel,
        out_shape=jax.ShapeDtypeStruct((STEPS, 4, SB, LAGS), F32),
        in_specs=[
            pl.BlockSpec(memory_space=pltpu.VMEM),
            pl.BlockSpec(memory_space=pltpu.SMEM),
            pl.BlockSpec(memory_space=pltpu.SMEM),
            pl.BlockSpec(memory_space=pl.ANY),
            pl.BlockSpec(memory_space=pl.ANY),
        ],
        out_specs=pl.BlockSpec(memory_space=pltpu.VMEM),
        scratch_shapes=[
            vmem(KQ, NFFT, QL),
            vmem(NFFT, LAGS),
            vmem(KQ, 256, QL, dtype=F32),
            vmem(2, 2, KQ, NZ, SB, PL),
            vmem(2 * NY, NZ, SB, PL),
            vmem(2 * NY, NZ, SB, PL),
            vmem(2, KQ, NZ, SB, PL),
            vmem(2, NZ, STEPS, SB, PL),
            *[vmem(NZ, n, SB, PL) for _, _, n in GROUPS],
            vmem(2, STEPS, KQ, NZ, SB, PL),
            vmem(3, NZ, 2 * SB, HALF, dtype=F32),
            vmem(3, NZ, SB, PB, dtype=F32),
            vmem(STEPS, 2 * SB * SB, NFFT),
            vmem(2, 8, 2, SB, LAGS, dtype=F32),
            vmem(STEPS, 2, 4, 2, SB, LAGS),
            vmem(STEPS, 2, 4, 2, SB, LAGS),
            vmem(STEPS, 2, 2, 4, SB, LAGS),
            vmem(STEPS, 3, 4, SB, LAGS),
            vmem(STEPS, 8, 2, SB, LAGS, dtype=F32),
            vmem(STEPS, 2, 2, 4, SB, LAGS, dtype=F32),
            dma(KQ + 1),
            dma(2, 7), dma(2, 7), dma(2),
            dma(6, NZ), dma(6, NZ),
            dma(6, NZ), dma(6, NZ),
            dma(6, NY), dma(6, NY),
            dma(4, STEPS), dma(4, STEPS),
        ],
        compiler_params=pltpu.CompilerParams(
            collective_id=0, has_side_effects=True, vmem_limit_bytes=56 * 2**20
        ),
        name="correlate",
    )(traces, valid_flags, source_block, jnp.asarray(dft_table()), jnp.asarray(lag_table()))


def solution(mesh):
    placed = (P("seg", None, "rcv", None), P(), P())
    return jax.shard_map(
        local, mesh=mesh, in_specs=placed, out_specs=P(None, "seg", "rcv", None), check_vma=False
    )
```
